512 devices in a mesh: dp: 16 (over y, core), ctx: 32 (over x, z).
Axes of the slice: x: 4, y: 8, z: 8, core: 2. Of those that a mesh axis runs over, the one named last changes fastest.
Arguments:
- queries: bfloat16 [65536, 4096], P(('dp', 'ctx')), may hold values from -8 to 8
- keys: bfloat16 [65536, 512], P(('dp', 'ctx')), may hold values from -8 to 8
- values: bfloat16 [65536, 512], P(('dp', 'ctx')), may hold values from -6 to 6
- outputs: bfloat16 [65536, 4096], P(('dp', 'ctx')), may hold values from -2 to 2
- out_grad: bfloat16 [65536, 4096], P(('dp', 'ctx')), may hold values from -96 to 96
- doc_start: int32 [16, 4096], replicated, may hold values from 0 to 3584, as said below
Outputs:
- q_grad: bfloat16 [65536, 4096], P(('dp', 'ctx'))
- key_gradient: bfloat16 [65536, 512], P(('dp', 'ctx'))
- value_gradient: bfloat16 [65536, 512], P(('dp', 'ctx'))
The draws below stay inside these ranges and needn't reach their ends.
Inputs may be any that keep to these rules, and one draw needn't show every extreme that they name: `doc_start`: Non-decreasing along each group, a multiple of 128, at most the position itself and equal to it where a document begins; documents are whole runs of 128-token units. Of the two groups g and g + 8, one holds two documents, of exactly 18 and 14 units in that order, and the other holds documents of 4 or 8 units, each beginning at a multiple of 4 units, its last 4 units being a document of their own.
All inputs are finite; a program needn't handle non-finite values.
Results may differ from the reference program's by a relative error of at most 0.013.
Values may be sent and summed in bfloat16 or wider, within the bound.
No kernel may reach another device: no remote copies, remote signals or barrier semaphores. Data moves between devices by JAX's collectives and lax.ppermute only.
A program may use at most 64 MiB of HBM per device.

```python
import jax
import jax.numpy as jnp
from jax import lax

QUERY_HEADS = 32
KEY_VALUE_HEADS = 4
HEAD_SIZE = 128
GROUP_TOKENS = 4096
DATA_GROUPS = 16
TOTAL_TOKENS = 65536
UNIT = 128


def draw_queries(key, part):
    key = jax.random.fold_in(key, 1)
    base_offset = jnp.clip(jax.random.normal(key, (TOTAL_TOKENS, QUERY_HEADS, HEAD_SIZE), jnp.float32), -6.0, 6.0)
    return base_offset.reshape(TOTAL_TOKENS, QUERY_HEADS * HEAD_SIZE).astype(jnp.bfloat16)


def draw_keys(key, part):
    key = jax.random.fold_in(key, 2)
    base_offset = jnp.clip(jax.random.normal(key, (TOTAL_TOKENS, KEY_VALUE_HEADS, HEAD_SIZE), jnp.float32), -6.0, 6.0)
    return base_offset.reshape(TOTAL_TOKENS, KEY_VALUE_HEADS * HEAD_SIZE).astype(jnp.bfloat16)


def draw_doc_start(key, part):
    key = jax.random.fold_in(key, 3)
    keys_list = jax.random.split(key, 4)
    half_groups = DATA_GROUPS // 2
    flips = jax.random.randint(keys_list[0], (half_groups,), 0, 2)
    heavy = jnp.concatenate([1 - flips, flips])
    units = jnp.arange(32, dtype=jnp.int32)[None, :]
    heavy_start = jnp.broadcast_to(jnp.where(units < 18, 0, 18), (DATA_GROUPS, 32))
    slots = units // 4
    coin = jax.random.randint(keys_list[3], (DATA_GROUPS, 8), 0, 2)
    slot_coin = jnp.repeat(coin, 4, axis=1)
    begins = (units % 4 == 0) & ((slots % 2 == 0) | (slot_coin == 1) | (slots == 7))
    light_start = lax.cummax(jnp.where(begins, units, 0), axis=1)
    start_unit = jnp.where(heavy[:, None] == 1, heavy_start, light_start)
    return (jnp.repeat(start_unit, UNIT, axis=1) * UNIT).astype(jnp.int32)


def steps_of(rng, shape, shards, low, high):
    loudness = 1.0
    for axis_at, blocks in shards:
        heights = jax.random.uniform(jax.random.fold_in(jax.random.fold_in(rng, 6), axis_at), (blocks,), jnp.float32, low / len(shards), high / len(shards))
        loudness = loudness * jnp.repeat(jnp.exp(heights), shape[axis_at] // blocks).reshape((-1,) + (1,) * (len(shape) - 1 - axis_at))
    return loudness


def gaussian(key, shape, scale, limit, pieces=(), kind=jnp.bfloat16):
    values = jax.random.normal(key, shape, jnp.float32) * scale
    if len(pieces) > 0:
        values = steps_of(key, shape, pieces, -0.22, 0.18) * values
    return jnp.clip(values, min=-limit, max=limit).astype(kind)


def setup_inputs(seed: int = 0) -> dict:
    arg_keys = jax.random.split(jax.random.key(seed), 7)
    queries = draw_queries(jax.random.fold_in(arg_keys[6], 71), 0)
    keys = draw_keys(jax.random.fold_in(arg_keys[6], 71), 0)
    values = gaussian(arg_keys[2], (TOTAL_TOKENS, KEY_VALUE_HEADS * HEAD_SIZE), 1.0, 6.0, ((0, 512),))
    outputs = gaussian(arg_keys[3], (TOTAL_TOKENS, QUERY_HEADS * HEAD_SIZE), 0.3, 2.0, ((0, 512),))
    out_grad = gaussian(arg_keys[4], (TOTAL_TOKENS, QUERY_HEADS * HEAD_SIZE), 16.0, 96.0, ((0, 512),))
    doc_start = draw_doc_start(jax.random.fold_in(arg_keys[6], 71), 0)
    return {"queries": queries, "keys": keys, "values": values, "outputs": outputs, "out_grad": out_grad, "doc_start": doc_start}


def tile_grads(query_tiles, grad_tiles, delta_tiles, key_rows, value_rows, doc_first, first_tile, tile_stride):
    tile_count, tile_rows, head_width = query_tiles.shape
    total_rows = key_rows.shape[0]
    key_cols = min(128, tile_rows)
    score_scale = head_width ** -0.5

    def one_tile(running_sums, payload):
        key_gradient_out, value_gradient_out = running_sums
        query_tile, grad_tile, delta_tile, number = payload
        row_zero = (first_tile + tile_stride * number) * tile_rows
        row_pos = row_zero + jnp.arange(tile_rows, dtype=jnp.int32)
        row_first = lax.dynamic_slice_in_dim(doc_first, row_zero, tile_rows)
        block_low = row_first[0] // key_cols
        block_high = (row_zero + tile_rows) // key_cols

        def scores(block_index):
            offset = block_index * key_cols
            key_block = lax.dynamic_slice_in_dim(key_rows, offset, key_cols)
            col_pos = offset + jnp.arange(key_cols, dtype=jnp.int32)
            allowed = (col_pos[None, :] >= row_first[:, None]) & (col_pos[None, :] <= row_pos[:, None])
            logits = jnp.dot(query_tile, key_block.T, preferred_element_type=jnp.float32) * score_scale
            return logits, allowed, key_block

        def running(block_index, loop_state):
            top_value, exp_total = loop_state
            logits, allowed, unused_block = scores(block_index)
            new_top = jnp.maximum(top_value, jnp.max(jnp.where(allowed, logits, -1e30), axis=1))
            shifted = jnp.where(allowed, jnp.exp(logits - new_top[:, None]), 0.0)
            exp_total = exp_total * jnp.exp(top_value - new_top) + jnp.sum(shifted, axis=1)
            return new_top, exp_total

        start_top = jnp.full((tile_rows,), -1e30, jnp.float32)
        start_total = jnp.zeros((tile_rows,), jnp.float32)
        top_value, exp_total = lax.fori_loop(block_low, block_high, running, (start_top, start_total))
        log_total = top_value + jnp.log(exp_total)

        def gradients(block_index, loop_state):
            query_acc, key_acc, value_acc = loop_state
            offset = block_index * key_cols
            logits, allowed, key_block = scores(block_index)
            value_block = lax.dynamic_slice_in_dim(value_rows, offset, key_cols)
            prob = jnp.where(allowed, jnp.exp(logits - log_total[:, None]), 0.0)
            dprob = jnp.dot(grad_tile, value_block.T, preferred_element_type=jnp.float32)
            dscore = (prob * (dprob - delta_tile[:, None])).astype(jnp.bfloat16)
            prob_low = prob.astype(jnp.bfloat16)
            value_add = jnp.dot(prob_low.T, grad_tile, preferred_element_type=jnp.float32)
            key_add = jnp.dot(dscore.T, query_tile, preferred_element_type=jnp.float32) * score_scale
            query_acc = query_acc + jnp.dot(dscore, key_block, preferred_element_type=jnp.float32)
            key_acc = lax.dynamic_update_slice_in_dim(key_acc, lax.dynamic_slice_in_dim(key_acc, offset, key_cols) + key_add, offset, 0)
            value_acc = lax.dynamic_update_slice_in_dim(value_acc, lax.dynamic_slice_in_dim(value_acc, offset, key_cols) + value_add, offset, 0)
            return query_acc, key_acc, value_acc

        start_query = jnp.zeros((tile_rows, head_width), jnp.float32)
        query_acc, key_gradient_out, value_gradient_out = lax.fori_loop(block_low, block_high, gradients, (start_query, key_gradient_out, value_gradient_out))
        return (key_gradient_out, value_gradient_out), query_acc * score_scale

    zero_rows = jnp.zeros((total_rows, head_width), jnp.float32)
    numbers = jnp.arange(tile_count, dtype=jnp.int32)
    (key_gradient_out, value_gradient_out), query_grad = lax.scan(one_tile, (zero_rows, zero_rows), (query_tiles, grad_tiles, delta_tiles, numbers))
    return query_grad, key_gradient_out, value_gradient_out


def reference(queries, keys, values, outputs, out_grad, doc_start):
    tile_rows = min(512, GROUP_TOKENS // 2)
    tile_count = GROUP_TOKENS // tile_rows
    heads_per_share = QUERY_HEADS // KEY_VALUE_HEADS

    def one_group(payload):
        query_group, key_group, value_group, output_group, grad_group, doc_first = payload

        def one_head(head_index):
            kv_index = head_index // heads_per_share
            query_head = query_group[:, head_index]
            output_head = output_group[:, head_index]
            grad_head = grad_group[:, head_index]
            key_head = key_group[:, kv_index]
            value_head = value_group[:, kv_index]
            row_delta = jnp.sum(grad_head.astype(jnp.float32) * output_head.astype(jnp.float32), axis=1)
            query_part, key_part, value_part = tile_grads(
                query_head.reshape(tile_count, tile_rows, HEAD_SIZE),
                grad_head.reshape(tile_count, tile_rows, HEAD_SIZE),
                row_delta.reshape(tile_count, tile_rows),
                key_head, value_head, doc_first, 0, 1)
            return (query_part.reshape(GROUP_TOKENS, HEAD_SIZE).astype(jnp.bfloat16),
                    key_part.astype(jnp.bfloat16), value_part.astype(jnp.bfloat16))

        query_heads, key_head_layout, value_head_layout = lax.map(one_head, jnp.arange(QUERY_HEADS, dtype=jnp.int32))
        query_grad = jnp.transpose(query_heads, (1, 0, 2)).reshape(GROUP_TOKENS, QUERY_HEADS * HEAD_SIZE)
        key_gradient_sum = jnp.sum(key_head_layout.astype(jnp.float32).reshape(KEY_VALUE_HEADS, heads_per_share, GROUP_TOKENS, HEAD_SIZE), axis=1).astype(jnp.bfloat16)
        value_gradient_sum = jnp.sum(value_head_layout.astype(jnp.float32).reshape(KEY_VALUE_HEADS, heads_per_share, GROUP_TOKENS, HEAD_SIZE), axis=1).astype(jnp.bfloat16)
        key_gradient_out = jnp.transpose(key_gradient_sum, (1, 0, 2)).reshape(GROUP_TOKENS, KEY_VALUE_HEADS * HEAD_SIZE)
        value_gradient_out = jnp.transpose(value_gradient_sum, (1, 0, 2)).reshape(GROUP_TOKENS, KEY_VALUE_HEADS * HEAD_SIZE)
        return query_grad, key_gradient_out, value_gradient_out

    stacked_parts = lax.map(one_group, (
        queries.reshape(DATA_GROUPS, GROUP_TOKENS, QUERY_HEADS, HEAD_SIZE),
        keys.reshape(DATA_GROUPS, GROUP_TOKENS, KEY_VALUE_HEADS, HEAD_SIZE),
        values.reshape(DATA_GROUPS, GROUP_TOKENS, KEY_VALUE_HEADS, HEAD_SIZE),
        outputs.reshape(DATA_GROUPS, GROUP_TOKENS, QUERY_HEADS, HEAD_SIZE),
        out_grad.reshape(DATA_GROUPS, GROUP_TOKENS, QUERY_HEADS, HEAD_SIZE),
        doc_start))
    return (stacked_parts[0].reshape(TOTAL_TOKENS, QUERY_HEADS * HEAD_SIZE),
            stacked_parts[1].reshape(TOTAL_TOKENS, KEY_VALUE_HEADS * HEAD_SIZE),
            stacked_parts[2].reshape(TOTAL_TOKENS, KEY_VALUE_HEADS * HEAD_SIZE))
```

```python
import jax
import jax.numpy as jnp
from jax import lax
from jax.experimental import pallas as pl
from jax.experimental.pallas import tpu as pltpu
from jax.sharding import Mesh
from jax.sharding import PartitionSpec as P

HEADS = 8
HEAD = 128
UNIT = 128
CHUNK = 256
MAX_CHUNKS = 9
SCALE = HEAD ** -0.5
LOG2E = 1.4426950408889634
F32 = jnp.float32
BF16 = jnp.bfloat16


def dot(a, b, dims=(((1,), (0,)), ((), ()))):
    return lax.dot_general(a, b, dims, preferred_element_type=F32)


def grads_kernel(info, qd_ref, kv_ref, dq_ref, dkv_ref, s_ref, e_ref, qt, qn, gt, gn, dqt, dk, dv, kt):
    z = info[0]
    rows = HEADS * UNIT
    dk[...] = jnp.zeros_like(dk)
    dv[...] = jnp.zeros_like(dv)
    lane = lax.broadcasted_iota(jnp.int32, (CHUNK, HEAD), 1)
    minus = jnp.where(lane < 3, -1.0, 0.0).astype(BF16)
    gt[128:256, :] = jnp.zeros((128, rows), BF16)

    def pair(ch, which):
        zz = (ch % 4) * 2
        xx = ch // 4
        return jnp.concatenate([kv_ref[zz, xx, which], kv_ref[zz + 1, xx, which]], axis=0)

    def one_tile(i, carry):
        unit = 8 * i + z
        lo = info[1 + i]
        hi = unit // 2
        for h in range(HEADS):
            cols = slice(h * HEAD, (h + 1) * HEAD)
            block = qd_ref[i, :, cols]
            qn[h * UNIT:(h + 1) * UNIT, :] = block
            qt[:, cols] = block.T
        def scores(ch):
            return dot(pair(ch, 0), qt[...])

        s = scores(hi)
        key = lax.broadcasted_iota(jnp.int32, (CHUNK, rows), 0)
        query = lax.broadcasted_iota(jnp.int32, (CHUNK, rows), 1) % UNIT + (unit % 2) * UNIT
        s = jnp.where(key <= query, s, -1e30)
        s_ref[hi - lo] = s
        top = jnp.max(s.reshape(CHUNK // 8, 8, rows), axis=0)

        def body1(ch, top):
            s = scores(ch)
            s_ref[ch - lo] = s
            return jnp.maximum(top, jnp.max(s.reshape(CHUNK // 8, 8, rows), axis=0))

        top = lax.fori_loop(lo, hi, body1, top)
        top = jnp.max(top, axis=0, keepdims=True) * (SCALE * LOG2E)

        def body2(j, total):
            e = jnp.exp2(s_ref[j] * (SCALE * LOG2E) - top)
            e_ref[j] = e.astype(BF16)
            return total + jnp.sum(e.reshape(CHUNK // 8, 8, rows), axis=0)

        total = lax.fori_loop(0, hi - lo + 1, body2, jnp.zeros((8, rows), F32))
        inv = 1.0 / jnp.sum(total, axis=0, keepdims=True)
        extra = qd_ref[i, :, 2 * rows:2 * rows + HEAD].astype(F32).T
        for h in range(HEADS):
            cols = slice(h * HEAD, (h + 1) * HEAD)
            inv_h = inv[:, cols]
            g = (qd_ref[i, :, rows + h * HEAD:rows + (h + 1) * HEAD].astype(F32).T * inv_h)
            gt[0:128, cols] = g.astype(BF16)
            gn[h * UNIT:(h + 1) * UNIT, :] = g.T.astype(BF16)
            delta = (extra[h:h + 1] + extra[8 + h:9 + h] + extra[16 + h:17 + h]) * inv_h
            d0 = delta.astype(BF16).astype(F32)
            d1 = (delta - d0).astype(BF16).astype(F32)
            d2 = delta - d0 - d1
            row = lax.broadcasted_iota(jnp.int32, (16, HEAD), 0)
            gt[128:144, cols] = jnp.where(row == 0, d0, jnp.where(row == 1, d1, jnp.where(row == 2, d2, 0.0))).astype(BF16)
        dqt[...] = jnp.zeros_like(dqt)

        def body3(ch, carry):
            e = e_ref[ch - lo]
            dv[ch] += dot(e, gn[...])
            dp = dot(jnp.concatenate([pair(ch, 1), minus], axis=1), gt[...])
            ds = e * dp.astype(BF16)
            dk[ch] += dot(ds, qn[...])
            dqt[...] += dot(pair(ch, 0), ds, (((0,), (0,)), ((), ())))
            return carry

        lax.fori_loop(lo, hi + 1, body3, 0)
        for h in range(HEADS):
            cols = slice(h * HEAD, (h + 1) * HEAD)
            dq_ref[i, :, cols] = (dqt[:, cols].T * SCALE).astype(BF16)
        return carry

    lax.fori_loop(0, 4, one_tile, 0)

    def flush(ch, carry):
        zz = (ch % 4) * 2
        xx = ch // 4
        for part in range(2):
            r = slice(part * UNIT, (part + 1) * UNIT)
            dkv_ref[zz + part, xx, 0] = (dk[ch, r, :] * SCALE).astype(BF16)
            dkv_ref[zz + part, xx, 1] = dv[ch, r, :].astype(BF16)
        return carry

    lax.fori_loop(0, 16, flush, 0)


def grads(info, qd, kv):
    rows = HEADS * UNIT
    vm = pl.BlockSpec(memory_space=pltpu.VMEM)
    return pl.pallas_call(
        grads_kernel,
        out_shape=(jax.ShapeDtypeStruct((4, UNIT, rows), BF16), jax.ShapeDtypeStruct((8, 4, 2, UNIT, HEAD), BF16)),
        in_specs=[pl.BlockSpec(memory_space=pltpu.SMEM), vm, vm],
        out_specs=(vm, vm),
        scratch_shapes=[
            pltpu.VMEM((MAX_CHUNKS, CHUNK, rows), F32),
            pltpu.VMEM((MAX_CHUNKS, CHUNK, rows), BF16),
            pltpu.VMEM((HEAD, rows), BF16),
            pltpu.VMEM((rows, HEAD), BF16),
            pltpu.VMEM((2 * HEAD, rows), BF16),
            pltpu.VMEM((rows, HEAD), BF16),
            pltpu.VMEM((HEAD, rows), F32),
            pltpu.VMEM((16, CHUNK, HEAD), F32),
            pltpu.VMEM((16, CHUNK, HEAD), F32),
            pltpu.VMEM((16, HEAD, CHUNK), BF16),
        ],
        compiler_params=pltpu.CompilerParams(vmem_limit_bytes=48 * 1024 * 1024),
        cost_estimate=pl.CostEstimate(flops=15_000_000_000, bytes_accessed=8_000_000, transcendentals=6_000_000),
    )(info, qd, kv)


def pack_keys_kernel(k_ref, v_ref, out_ref):
    for c in range(4):
        cols = slice(c * HEAD, (c + 1) * HEAD)
        out_ref[c, 0] = k_ref[:, cols]
        out_ref[c, 1] = v_ref[:, cols]


def pack_keys(keys, values):
    vm = pl.BlockSpec(memory_space=pltpu.VMEM)
    return pl.pallas_call(
        pack_keys_kernel,
        out_shape=jax.ShapeDtypeStruct((4, 2, UNIT, HEAD), BF16),
        in_specs=[vm, vm],
        out_specs=vm,
    )(keys, values)


def pack_queries_kernel(q_ref, o_ref, g_ref, out_ref):
    rows = HEADS * HEAD
    lane = lax.broadcasted_iota(jnp.int32, (UNIT, HEAD), 1)
    for c in range(4):
        out_ref[c, :, 0:rows] = q_ref[:, c * rows:(c + 1) * rows]
        out_ref[c, :, rows:2 * rows] = g_ref[:, c * rows:(c + 1) * rows]
        delta = jnp.zeros((UNIT, HEAD), F32)
        for h in range(HEADS):
            cols = slice(c * rows + h * HEAD, c * rows + (h + 1) * HEAD)
            one = jnp.sum(g_ref[:, cols].astype(F32) * o_ref[:, cols].astype(F32), axis=1, keepdims=True)
            delta = jnp.where(lane % HEADS == h, one, delta)
        first = delta.astype(BF16).astype(F32)
        second = (delta - first).astype(BF16).astype(F32)
        third = delta - first - second
        parts = jnp.where(lane < 8, first, jnp.where(lane < 16, second, jnp.where(lane < 24, third, 0.0)))
        out_ref[c, :, 2 * rows:2 * rows + HEAD] = parts.astype(BF16)


def pack_queries(queries, outputs, out_grad):
    vm = pl.BlockSpec(memory_space=pltpu.VMEM)
    return pl.pallas_call(
        pack_queries_kernel,
        out_shape=jax.ShapeDtypeStruct((4, UNIT, 2 * HEADS * HEAD + HEAD), BF16),
        in_specs=[vm, vm, vm],
        out_specs=vm,
        compiler_params=pltpu.CompilerParams(vmem_limit_bytes=16 * 1024 * 1024),
    )(queries, outputs, out_grad)


def on_device(queries, keys, values, outputs, out_grad, doc_start):
    z = lax.axis_index("z")
    own_start = lax.dynamic_index_in_dim(doc_start, lax.axis_index("dp"), 0, keepdims=False)
    first_chunk = own_start.reshape(4, 8, UNIT)[:, :, 0] // CHUNK
    first_chunk = lax.dynamic_index_in_dim(first_chunk, z, 1, keepdims=False)
    info = jnp.concatenate([z[None].astype(jnp.int32), first_chunk])
    kv = lax.all_to_all(pack_keys(keys, values), "x", 0, 0, tiled=True)
    kv = lax.all_gather(kv, "z", axis=0)
    qd = lax.all_to_all(pack_queries(queries, outputs, out_grad), "x", 0, 0, tiled=True)
    dq, dkv = grads(info, qd, kv)
    dq = lax.all_to_all(dq, "x", 0, 0, tiled=True)
    q_grad = jnp.moveaxis(dq, 0, 1).reshape(UNIT, 4 * HEADS * HEAD)
    dkv = lax.psum_scatter(dkv, "z", scatter_dimension=0)
    dkv = lax.all_to_all(dkv, "x", 0, 0, tiled=True)
    dkv = jnp.moveaxis(dkv, 0, 2).reshape(2, UNIT, 4 * HEAD)
    return q_grad, dkv[0], dkv[1]


def solution(mesh):
    split = Mesh(mesh.devices.reshape(16, 4, 8), ("dp", "x", "z"))
    rows = P(("dp", "x", "z"), None)
    return jax.shard_map(
        on_device,
        mesh=split,
        in_specs=(rows, rows, rows, rows, rows, P()),
        out_specs=(rows, rows, rows),
        check_vma=False,
    )
```

```python
import jax
import jax.numpy as jnp
from jax import lax
from jax.experimental import pallas as pl
from jax.experimental.pallas import tpu as pltpu
from jax.sharding import Mesh
from jax.sharding import PartitionSpec as P

HEADS = 8
HEAD = 128
UNIT = 128
ROWS = HEADS * UNIT
WIDE = 2 * ROWS + HEAD
CHUNK = 256
CHUNKS = 16
MAX_CHUNKS = 9
SCALE = HEAD**-0.5
VMEM_LIMIT = 63 * 1024 * 1024
LOG2E = 1.4426950408889634
F32 = jnp.float32
BF16 = jnp.bfloat16
NN = (((1,), (0,)), ((), ()))
NT = (((1,), (1,)), ((), ()))
ANY = pl.BlockSpec(memory_space=pl.ANY)
VM = pl.BlockSpec(memory_space=pltpu.VMEM)
SM = pl.BlockSpec(memory_space=pltpu.SMEM)


def dot(a, b, dims=NN):
    return lax.dot_general(a, b, dims, preferred_element_type=F32)


def pairwise(lo, hi, body):
    def two(t, carry):
        body((lo + 2 * t, lo + 2 * t + 1))
        return carry

    def last(t, carry):
        body((hi - 1,))
        return carry

    n = hi - lo
    lax.fori_loop(0, n // 2, two, 0)
    lax.fori_loop(0, n % 2, last, 0)


def pack_keys_kernel(k_ref, v_ref, out_ref):
    for c in range(4):
        for n, ref in enumerate((k_ref, v_ref)):
            block = ref[:, c * HEAD : (c + 1) * HEAD].astype(F32)
            peak = jnp.max(jnp.max(jnp.abs(block), axis=1, keepdims=True), axis=0, keepdims=True)
            power = jnp.where(peak > 0, 13.0 - jnp.floor(jnp.log2(peak)), 0.0)
            power = jnp.broadcast_to(jnp.minimum(power, 120.0), (8, HEAD))
            out_ref[c, n * UNIT : (n + 1) * UNIT, :] = (block * jnp.exp2(power)[0:1, :]).astype(BF16)
            if n == 0:
                first = power
        out_ref[c, 2 * UNIT : 2 * UNIT + 16, :] = jnp.concatenate([first, power], axis=0).astype(BF16)


def pack_keys(keys, values):
    return pl.pallas_call(
        pack_keys_kernel,
        out_shape=jax.ShapeDtypeStruct((4, 2 * UNIT + 16, HEAD), BF16),
        in_specs=[VM, VM],
        out_specs=VM,
    )(keys, values)


def unpack(gathered, n):
    block = gathered[:, :, n * UNIT : (n + 1) * UNIT, :].astype(F32)
    power = gathered[:, :, 2 * UNIT + 8 * n : 2 * UNIT + 8 * n + 1, :].astype(F32)
    return (block * jnp.exp2(-power)).astype(BF16)


def pack_kernel(q_ref, o_ref, g_ref, out_ref):
    lane = lax.broadcasted_iota(jnp.int32, (UNIT, HEAD), 1)
    for c in range(4):
        base = c * ROWS
        out_ref[c, :, 0:ROWS] = q_ref[:, base : base + ROWS]
        out_ref[c, :, ROWS : 2 * ROWS] = g_ref[:, base : base + ROWS]
        delta = jnp.zeros((UNIT, HEAD), F32)
        for h in range(HEADS):
            cols = slice(base + h * HEAD, base + (h + 1) * HEAD)
            one = jnp.sum(g_ref[:, cols].astype(F32) * o_ref[:, cols].astype(F32), axis=1, keepdims=True)
            delta = jnp.where(lane % HEADS == h, one, delta)
        first = delta.astype(BF16).astype(F32)
        second = (delta - first).astype(BF16).astype(F32)
        third = delta - first - second
        parts = jnp.where(lane < 8, first, jnp.where(lane < 16, second, jnp.where(lane < 24, third, 0.0)))
        out_ref[c, :, 2 * ROWS : WIDE] = parts.astype(BF16)


def pack(queries, outputs, out_grad):
    return pl.pallas_call(
        pack_kernel,
        out_shape=jax.ShapeDtypeStruct((4, UNIT, WIDE), BF16),
        in_specs=[VM, VM, VM],
        out_specs=VM,
        compiler_params=pltpu.CompilerParams(vmem_limit_bytes=16 * 1024 * 1024),
        cost_estimate=pl.CostEstimate(flops=2_000_000, bytes_accessed=5_000_000, transcendentals=0),
    )(queries, outputs, out_grad)


def load_units(ref, into, sems, columns=None):
    copies = []
    for z in range(8):
        target = into.at[:, z] if columns is None else into.at[:, z, :, columns]
        copies.append(pltpu.make_async_copy(ref.at[z], target, sems.at[z]))
        copies[z].start()
    return copies


def chunk(ref, ch):
    block = ref[ch // 4, pl.ds((ch % 4) * 2, 2)]
    return block.reshape(CHUNK, block.shape[-1])


def load_parts(parts, into, sems):
    def copy(i):
        return pltpu.make_async_copy(parts.at[i], into.at[i], sems.at[i])

    for i in (3, 2, 1, 0):
        copy(i).start()
    return copy


def value_kernel(info, p_ref, k_ref, dv_ref, lse_ref, part, key, s_ref, e_ref, qt, gn, dv, out, top_ref, sum_ref, in_sems, key_sems, out_sems):
    z = info[1]
    load_key = load_units(k_ref, key, key_sems)
    load_part = load_parts(p_ref, part, in_sems)
    dv[...] = jnp.zeros_like(dv)
    for copy in load_key:
        copy.wait()

    def put(ch):
        return pltpu.make_async_copy(out.at[ch], dv_ref.at[ch], out_sems.at[ch])

    def one_tile(t, carry):
        i = 3 - t
        unit = 8 * i + z
        lo = info[2 + i]
        hi = unit // 2
        load_part(i).wait()
        for h in range(HEADS):
            cols = slice(h * HEAD, (h + 1) * HEAD)
            qt[:, cols] = part[i, :, cols].T

        s = dot(chunk(key, hi), qt[...])
        row = lax.broadcasted_iota(jnp.int32, (CHUNK, ROWS), 0)
        query = lax.broadcasted_iota(jnp.int32, (CHUNK, ROWS), 1) % UNIT + (unit % 2) * UNIT
        s = jnp.where(row <= query, s, -1e30)
        s_ref[hi - lo] = s
        top_ref[...] = jnp.max(s.reshape(CHUNK // 8, 8, ROWS), axis=0)

        def highest(chs):
            top = top_ref[...]
            ss = [dot(chunk(key, ch), qt[...]) for ch in chs]
            for ch, s in zip(chs, ss):
                s_ref[ch - lo] = s
                top = jnp.maximum(top, jnp.max(s.reshape(CHUNK // 8, 8, ROWS), axis=0))
            top_ref[...] = top

        pairwise(lo, hi, highest)
        top = jnp.max(top_ref[...], axis=0, keepdims=True) * (SCALE * LOG2E)
        sum_ref[...] = jnp.zeros_like(sum_ref)

        def powers(js):
            total = sum_ref[...]
            for j in js:
                e = jnp.exp2(s_ref[j] * (SCALE * LOG2E) - top)
                e_ref[j] = e.astype(BF16)
                total = total + jnp.sum(e.reshape(CHUNK // 8, 8, ROWS), axis=0)
            sum_ref[...] = total

        pairwise(0, hi - lo + 1, powers)
        total = jnp.sum(sum_ref[...], axis=0, keepdims=True)
        lse = top + jnp.log2(total)
        inv = 1.0 / total
        for h in range(HEADS):
            cols = slice(h * HEAD, (h + 1) * HEAD)
            lse_ref[i, h : h + 1, :] = lse[:, cols]
            column = jnp.broadcast_to(inv[:, cols], (UNIT, HEAD)).T
            grad = part[i, :, ROWS + h * HEAD : ROWS + (h + 1) * HEAD].astype(F32)
            gn[h * UNIT : (h + 1) * UNIT, :] = (grad * column).astype(BF16)

        def add(chs):
            for ch in chs:
                dv[ch] += dot(e_ref[ch - lo], gn[...])

        pairwise(lo, hi + 1, add)

        def flush(ch, carry):
            out[ch] = dv[ch].astype(BF16)
            put(ch).start()
            return carry

        lax.fori_loop(4 * i, 4 * i + 4, flush, 0)
        return carry

    lax.fori_loop(0, 4, one_tile, 0)

    def finish(ch, carry):
        put(ch).wait()
        return carry

    lax.fori_loop(0, CHUNKS, finish, 0)


def value_grads(info, parts, key):
    return pl.pallas_call(
        value_kernel,
        out_shape=(jax.ShapeDtypeStruct((CHUNKS, CHUNK, HEAD), BF16), jax.ShapeDtypeStruct((4, HEADS, UNIT), F32)),
        in_specs=[SM, ANY, ANY],
        out_specs=(ANY, VM),
        scratch_shapes=[
            pltpu.VMEM((4, UNIT, WIDE), BF16),
            pltpu.VMEM((4, 8, UNIT, HEAD), BF16),
            pltpu.VMEM((MAX_CHUNKS, CHUNK, ROWS), F32),
            pltpu.VMEM((MAX_CHUNKS, CHUNK, ROWS), BF16),
            pltpu.VMEM((HEAD, ROWS), BF16),
            pltpu.VMEM((ROWS, HEAD), BF16),
            pltpu.VMEM((CHUNKS, CHUNK, HEAD), F32),
            pltpu.VMEM((CHUNKS, CHUNK, HEAD), BF16),
            pltpu.VMEM((8, ROWS), F32),
            pltpu.VMEM((8, ROWS), F32),
            pltpu.SemaphoreType.DMA((4,)),
            pltpu.SemaphoreType.DMA((8,)),
            pltpu.SemaphoreType.DMA((CHUNKS,)),
        ],
        compiler_params=pltpu.CompilerParams(vmem_limit_bytes=VMEM_LIMIT),
        cost_estimate=pl.CostEstimate(flops=7_000_000_000, bytes_accessed=5_000_000, transcendentals=6_000_000),
    )(info, parts, key)


def key_kernel(info, p_ref, k_ref, v_ref, lse_ref, q0, q1, q2, q3, dk_ref, part, key, value, qn, qt, gn, lse, dq, dqs, dk, out, in_sems, key_sems, value_sems, out_sems, q_sems):
    x = info[0]
    z = info[1]
    load_key = load_units(k_ref, key, key_sems)
    load_value = load_units(v_ref, value, value_sems, pl.ds(0, HEAD))
    load_part = load_parts(p_ref, part, in_sems)
    dk[...] = jnp.zeros_like(dk)

    def minus(ch, carry):
        value[ch // 8, ch % 8, :, HEAD : 2 * HEAD] = jnp.full((UNIT, HEAD), -1.0, BF16)
        return carry

    lax.fori_loop(0, 2 * CHUNKS, minus, 0)
    for copy in load_key + load_value:
        copy.wait()
    lane = lax.broadcasted_iota(jnp.int32, (UNIT, HEAD), 1)

    def put(unit):
        return pltpu.make_async_copy(out.at[unit], dk_ref.at[unit], out_sems.at[unit])

    def one_tile(t, carry):
        i = 3 - t
        unit = 8 * i + z
        lo = info[2 + i]
        hi = unit // 2
        load_part(i).wait()
        extra = part[i, :, 2 * ROWS : WIDE]
        for h in range(HEADS):
            rows = slice(h * UNIT, (h + 1) * UNIT)
            block = part[i, :, h * HEAD : (h + 1) * HEAD]
            qn[rows, :] = block
            qt[:, rows] = block.T
            gn[rows, 0:HEAD] = part[i, :, ROWS + h * HEAD : ROWS + (h + 1) * HEAD]
            gn[rows, HEAD : 2 * HEAD] = jnp.where(lane % HEADS == h, extra, jnp.zeros_like(extra))
            lse[rows, :] = jnp.broadcast_to(lse_ref[i, h : h + 1, :], (UNIT, HEAD)).T
        dq[...] = jnp.zeros_like(dq)

        def gradients(chs, mask=False):
            ss = [dot(qn[...], chunk(key, ch), NT) for ch in chs]
            dps = [dot(gn[...], chunk(value, ch), NT).astype(BF16) for ch in chs]
            if mask:
                row = lax.broadcasted_iota(jnp.int32, (ROWS, CHUNK), 0) % UNIT + (unit % 2) * UNIT
                col = lax.broadcasted_iota(jnp.int32, (ROWS, CHUNK), 1)
                ss = [jnp.where(col <= row, s, -1e30) for s in ss]
            total = None
            for ch, s, dp in zip(chs, ss, dps):
                both = jnp.concatenate([lse[...], lse[...]], axis=1)
                ds = jnp.exp2(s * (SCALE * LOG2E) - both).astype(BF16) * dp
                dk[ch] += dot(qt[...], ds)
                one = dot(ds, chunk(key, ch))
                total = one if total is None else total + one
            dq[...] += total

        gradients((hi,), True)
        pairwise(lo, hi, gradients)
        for h in range(HEADS):
            dqs[i, :, h * HEAD : (h + 1) * HEAD] = (dq[h * UNIT : (h + 1) * UNIT, :] * SCALE).astype(BF16)

        def flush(ch, carry):
            for half in range(2):
                out[2 * ch + half] = (dk[ch, :, half * UNIT : (half + 1) * UNIT] * SCALE).astype(BF16)
                put(2 * ch + half).start()
            return carry

        lax.fori_loop(4 * i, 4 * i + 4, flush, 0)
        return carry

    lax.fori_loop(0, 4, one_tile, 0)
    copies = []
    for s, ref in enumerate((q0, q1, q2, q3)):
        copies.append(pltpu.make_async_copy(dqs.at[lax.rem(x + s, 4)], ref, q_sems.at[s]))
        copies[s].start()
    for copy in copies:
        copy.wait()

    def finish(unit, carry):
        put(unit).wait()
        return carry

    lax.fori_loop(0, 2 * CHUNKS, finish, 0)


def key_grads(info, parts, key, value, lse):
    one = jax.ShapeDtypeStruct((UNIT, ROWS), BF16)
    return pl.pallas_call(
        key_kernel,
        out_shape=[one] * 4 + [jax.ShapeDtypeStruct((2 * CHUNKS, HEAD, UNIT), BF16)],
        in_specs=[SM, ANY, ANY, ANY, VM],
        out_specs=[ANY] * 5,
        scratch_shapes=[
            pltpu.VMEM((4, UNIT, WIDE), BF16),
            pltpu.VMEM((4, 8, UNIT, HEAD), BF16),
            pltpu.VMEM((4, 8, UNIT, 2 * HEAD), BF16),
            pltpu.VMEM((ROWS, HEAD), BF16),
            pltpu.VMEM((HEAD, ROWS), BF16),
            pltpu.VMEM((ROWS, 2 * HEAD), BF16),
            pltpu.VMEM((ROWS, HEAD), F32),
            pltpu.VMEM((ROWS, HEAD), F32),
            pltpu.VMEM((4, UNIT, ROWS), BF16),
            pltpu.VMEM((CHUNKS, HEAD, CHUNK), F32),
            pltpu.VMEM((2 * CHUNKS, HEAD, UNIT), BF16),
            pltpu.SemaphoreType.DMA((4,)),
            pltpu.SemaphoreType.DMA((8,)),
            pltpu.SemaphoreType.DMA((8,)),
            pltpu.SemaphoreType.DMA((2 * CHUNKS,)),
            pltpu.SemaphoreType.DMA((4,)),
        ],
        compiler_params=pltpu.CompilerParams(vmem_limit_bytes=VMEM_LIMIT),
        cost_estimate=pl.CostEstimate(flops=9_000_000_000, bytes_accessed=6_000_000, transcendentals=6_000_000),
    )(info, parts, key, value, lse)


def add_senders(in_ref, out_ref, parts, sems, transposed):
    for c in range(4):
        pltpu.make_async_copy(in_ref.at[pl.ds(8 * c, 8)], parts.at[c], sems.at[c]).wait()
        total = parts[c, 0].astype(F32)
        for t in range(1, 8):
            total = total + parts[c, t].astype(F32)
        if transposed:
            total = total.T
        out_ref[:, c * HEAD : (c + 1) * HEAD] = total.astype(BF16)


def start_senders(in_ref, parts, sems):
    for c in range(4):
        pltpu.make_async_copy(in_ref.at[pl.ds(8 * c, 8)], parts.at[c], sems.at[c]).start()


def sum_kernel(in_ref, out_ref, parts, sems):
    start_senders(in_ref, parts, sems)
    add_senders(in_ref, out_ref, parts, sems, False)


def sum_senders(parts):
    return pl.pallas_call(
        sum_kernel,
        out_shape=jax.ShapeDtypeStruct((UNIT, 4 * HEAD), BF16),
        in_specs=[ANY],
        out_specs=VM,
        scratch_shapes=[pltpu.VMEM((4, 8, UNIT, HEAD), BF16), pltpu.SemaphoreType.DMA((4,))],
        cost_estimate=pl.CostEstimate(flops=1_000_000, bytes_accessed=1_200_000, transcendentals=0),
    )(parts)


def finish_kernel(info, q0, q1, q2, q3, dk_ref, q_ref, out_ref, whole, parts, q_sems, out_sems, sems):
    def place(s):
        return whole.at[:, pl.ds(pl.multiple_of(lax.rem(info[0] + 4 - s, 4) * ROWS, ROWS), ROWS)]

    def put(s):
        base = pl.multiple_of(lax.rem(info[0] + 4 - s, 4) * ROWS, ROWS)
        return pltpu.make_async_copy(place(s), q_ref.at[:, pl.ds(base, ROWS)], out_sems.at[s])

    takes = [pltpu.make_async_copy(ref, place(s), q_sems.at[s]) for s, ref in enumerate((q0, q1, q2, q3))]
    for take in takes:
        take.start()
    start_senders(dk_ref, parts, sems)
    for s in range(4):
        takes[s].wait()
        put(s).start()
    add_senders(dk_ref, out_ref, parts, sems, True)
    for s in range(4):
        put(s).wait()


def finish(info, dq, dk):
    return pl.pallas_call(
        finish_kernel,
        out_shape=(jax.ShapeDtypeStruct((UNIT, 4 * ROWS), BF16), jax.ShapeDtypeStruct((UNIT, 4 * HEAD), BF16)),
        in_specs=[SM] + [ANY] * 5,
        out_specs=(ANY, VM),
        scratch_shapes=[
            pltpu.VMEM((UNIT, 4 * ROWS), BF16),
            pltpu.VMEM((4, 8, UNIT, HEAD), BF16),
            pltpu.SemaphoreType.DMA((4,)),
            pltpu.SemaphoreType.DMA((4,)),
            pltpu.SemaphoreType.DMA((4,)),
        ],
        cost_estimate=pl.CostEstimate(flops=1_000_000, bytes_accessed=3_000_000, transcendentals=0),
    )(info, *dq, dk)


def shift(array, by):
    return lax.ppermute(array, "x", [(i, (i + by) % 4) for i in range(4)])


def exchange(parts):
    return [parts[0]] + [shift(parts[s], s) for s in (1, 2, 3)]


def to_all(array):
    return lax.all_to_all(array, ("x", "z"), 0, 0, tiled=True)


def on_device(queries, keys, values, outputs, out_grad, doc_start):
    x = lax.axis_index("x")
    z = lax.axis_index("z")
    own_start = lax.dynamic_index_in_dim(doc_start, lax.axis_index("dp"), 0, keepdims=False)
    first_chunk = own_start.reshape(4, 8, UNIT)[:, :, 0] // CHUNK
    first_chunk = lax.dynamic_index_in_dim(first_chunk, z, 1, keepdims=False)
    info = jnp.concatenate([x[None].astype(jnp.int32), z[None].astype(jnp.int32), first_chunk])

    kv = lax.all_to_all(pack_keys(keys, values).astype(jnp.float16), "x", 0, 0, tiled=True)
    parts = lax.all_to_all(pack(queries, outputs, out_grad), "x", 0, 0, tiled=True)
    kv = lax.all_gather(kv, "z", axis=0)
    key, value = unpack(kv, 0), unpack(kv, 1)
    dv, lse = value_grads(info, parts, key)
    dv = to_all(dv.reshape(32, UNIT, HEAD))
    *dq, dk = key_grads(info, parts, key, value, lse)
    dk, dv = lax.optimization_barrier((dk, dv))
    dk = to_all(dk)
    dq = exchange(dq)
    value_gradient = sum_senders(dv)
    dq, value_gradient = lax.optimization_barrier((dq, value_gradient))
    q_grad, key_gradient = finish(info, dq, dk)
    return q_grad, key_gradient, value_gradient


def solution(mesh):
    split = Mesh(mesh.devices.reshape(16, 4, 8), ("dp", "x", "z"))
    rows = P(("dp", "x", "z"), None)
    return jax.shard_map(
        on_device,
        mesh=split,
        in_specs=(rows, rows, rows, rows, rows, P()),
        out_specs=(rows, rows, rows),
        check_vma=False,
    )
```

```python
import jax
import jax.numpy as jnp
from jax import lax
from jax.experimental import pallas as pl
from jax.experimental.pallas import tpu as pltpu
from jax.sharding import Mesh
from jax.sharding import PartitionSpec as P

HEADS = 8
HEAD = 128
UNIT = 128
ROWS = HEADS * UNIT
WIDE = 2 * ROWS + HEAD
CHUNK = 256
CHUNKS = 16
MAX_CHUNKS = 9
SCALE = HEAD**-0.5
VMEM_LIMIT = 63 * 1024 * 1024
LOG2E = 1.4426950408889634
F32 = jnp.float32
BF16 = jnp.bfloat16
NN = (((1,), (0,)), ((), ()))
NT = (((1,), (1,)), ((), ()))
ANY = pl.BlockSpec(memory_space=pl.ANY)
VM = pl.BlockSpec(memory_space=pltpu.VMEM)
SM = pl.BlockSpec(memory_space=pltpu.SMEM)


def dot(a, b, dims=NN):
    return lax.dot_general(a, b, dims, preferred_element_type=F32)


def pairwise(lo, hi, body):
    def two(t, carry):
        body((lo + 2 * t, lo + 2 * t + 1))
        return carry

    def last(t, carry):
        body((hi - 1,))
        return carry

    n = hi - lo
    lax.fori_loop(0, n // 2, two, 0)
    lax.fori_loop(0, n % 2, last, 0)


def pack_keys_kernel(k_ref, v_ref, out_ref):
    for c in range(4):
        for n, ref in enumerate((k_ref, v_ref)):
            block = ref[:, c * HEAD : (c + 1) * HEAD].astype(F32)
            peak = jnp.max(jnp.max(jnp.abs(block), axis=1, keepdims=True), axis=0, keepdims=True)
            power = jnp.where(peak > 0, 13.0 - jnp.floor(jnp.log2(peak)), 0.0)
            power = jnp.broadcast_to(jnp.minimum(power, 120.0), (8, HEAD))
            out_ref[c, n * UNIT : (n + 1) * UNIT, :] = (block * jnp.exp2(power)[0:1, :]).astype(BF16)
            if n == 0:
                first = power
        out_ref[c, 2 * UNIT : 2 * UNIT + 16, :] = jnp.concatenate([first, power], axis=0).astype(BF16)


def pack_keys(keys, values):
    return pl.pallas_call(
        pack_keys_kernel,
        out_shape=jax.ShapeDtypeStruct((4, 2 * UNIT + 16, HEAD), BF16),
        in_specs=[VM, VM],
        out_specs=VM,
        compiler_params=pltpu.CompilerParams(vmem_limit_bytes=8 * 1024 * 1024),
    )(keys, values)


def unpack(gathered, n):
    block = gathered[:, :, n * UNIT : (n + 1) * UNIT, :].astype(F32)
    power = gathered[:, :, 2 * UNIT + 8 * n : 2 * UNIT + 8 * n + 1, :].astype(F32)
    return (block * jnp.exp2(-power)).astype(BF16)


def pack_kernel(q_ref, o_ref, g_ref, out_ref):
    lane = lax.broadcasted_iota(jnp.int32, (UNIT, HEAD), 1)
    for c in range(4):
        base = c * ROWS
        out_ref[c, :, 0:ROWS] = q_ref[:, base : base + ROWS]
        out_ref[c, :, ROWS : 2 * ROWS] = g_ref[:, base : base + ROWS]
        delta = jnp.zeros((UNIT, HEAD), F32)
        for h in range(HEADS):
            cols = slice(base + h * HEAD, base + (h + 1) * HEAD)
            one = jnp.sum(g_ref[:, cols].astype(F32) * o_ref[:, cols].astype(F32), axis=1, keepdims=True)
            delta = jnp.where(lane % HEADS == h, one, delta)
        first = delta.astype(BF16).astype(F32)
        second = (delta - first).astype(BF16).astype(F32)
        third = delta - first - second
        parts = jnp.where(lane < 8, first, jnp.where(lane < 16, second, jnp.where(lane < 24, third, 0.0)))
        out_ref[c, :, 2 * ROWS : WIDE] = parts.astype(BF16)


def pack(queries, outputs, out_grad):
    return pl.pallas_call(
        pack_kernel,
        out_shape=jax.ShapeDtypeStruct((4, UNIT, WIDE), BF16),
        in_specs=[VM, VM, VM],
        out_specs=VM,
        compiler_params=pltpu.CompilerParams(vmem_limit_bytes=16 * 1024 * 1024),
        cost_estimate=pl.CostEstimate(flops=2_000_000, bytes_accessed=5_000_000, transcendentals=0),
    )(queries, outputs, out_grad)


def load_parts(parts, into, sems):
    def copy(i):
        return pltpu.make_async_copy(parts.at[i], into.at[i], sems.at[i])

    for i in (3, 2, 1, 0):
        copy(i).start()
    return copy


def load_units(ref, into, sems, columns=None):
    copies = []
    for unit in range(2 * CHUNKS):
        target = into.at[unit] if columns is None else into.at[unit, :, columns]
        copies.append(pltpu.make_async_copy(ref.at[unit % 8, unit // 8], target, sems.at[unit]))
        copies[unit].start()
    return copies


def chunks(ref, at, count=1):
    return ref[pl.ds(2 * at, 2 * count)].reshape(count * CHUNK, ref.shape[-1])


def grouped(lo, hi, body, most):
    at = lo
    while most:

        def one(t, carry, at=at, most=most):
            body(at + most * t, most)
            return carry

        times = (hi - at) // most
        lax.fori_loop(0, times, one, 0)
        at = at + most * times
        most //= 2


def value_kernel(info, p_ref, k_ref, dv_ref, lse_ref, part, key, s_ref, e_ref, qt, gn, dv, out, top_ref, sum_ref, in_sems, key_sems, out_sems):
    z = info[1]
    load_key = load_units(k_ref, key, key_sems)
    load_part = load_parts(p_ref, part, in_sems)
    dv[...] = jnp.zeros_like(dv)
    for copy in load_key:
        copy.wait()

    def put(ch):
        return pltpu.make_async_copy(out.at[ch], dv_ref.at[ch], out_sems.at[ch])

    def one_tile(t, carry):
        i = 3 - t
        unit = 8 * i + z
        lo = info[2 + i]
        hi = unit // 2
        load_part(i).wait()
        for h in range(HEADS):
            cols = slice(h * HEAD, (h + 1) * HEAD)
            qt[:, cols] = part[i, :, cols].T

        s = dot(chunks(key, hi), qt[...])
        row = lax.broadcasted_iota(jnp.int32, (CHUNK, ROWS), 0)
        query = lax.broadcasted_iota(jnp.int32, (CHUNK, ROWS), 1) % UNIT + (unit % 2) * UNIT
        s = jnp.where(row <= query, s, -1e30)
        s_ref[hi - lo] = s
        top_ref[...] = jnp.max(s.reshape(CHUNK // 8, 8, ROWS), axis=0)

        def highest(at, count):
            s = dot(chunks(key, at, count), qt[...])
            s_ref[pl.ds(at - lo, count)] = s.reshape(count, CHUNK, ROWS)
            top_ref[...] = jnp.maximum(top_ref[...], jnp.max(s.reshape(count * CHUNK // 8, 8, ROWS), axis=0))

        grouped(lo, hi, highest, 2)
        top = jnp.max(top_ref[...], axis=0, keepdims=True) * (SCALE * LOG2E)
        sum_ref[...] = jnp.zeros_like(sum_ref)

        def powers(js):
            total = sum_ref[...]
            for j in js:
                e = jnp.exp2(s_ref[j] * (SCALE * LOG2E) - top)
                e_ref[j] = e.astype(BF16)
                total = total + jnp.sum(e.reshape(CHUNK // 8, 8, ROWS), axis=0)
            sum_ref[...] = total

        pairwise(0, hi - lo + 1, powers)
        total = jnp.sum(sum_ref[...], axis=0, keepdims=True)
        lse = top + jnp.log2(total)
        inv = 1.0 / total
        for h in range(HEADS):
            cols = slice(h * HEAD, (h + 1) * HEAD)
            lse_ref[i, h : h + 1, :] = lse[:, cols]
            column = jnp.broadcast_to(inv[:, cols], (UNIT, HEAD)).T
            grad = part[i, :, ROWS + h * HEAD : ROWS + (h + 1) * HEAD].astype(F32)
            gn[h * UNIT : (h + 1) * UNIT, :] = (grad * column).astype(BF16)

        def add(at, count):
            e = e_ref[pl.ds(at - lo, count)].reshape(count * CHUNK, ROWS)
            dv[pl.ds(at, count)] += dot(e, gn[...]).reshape(count, CHUNK, HEAD)

        grouped(lo, hi + 1, add, 4)

        def flush(ch, carry):
            out[ch] = dv[ch].astype(BF16)
            put(ch).start()
            return carry

        lax.fori_loop(4 * i, 4 * i + 4, flush, 0)
        return carry

    lax.fori_loop(0, 4, one_tile, 0)

    def finish(ch, carry):
        put(ch).wait()
        return carry

    lax.fori_loop(0, CHUNKS, finish, 0)


def value_grads(info, parts, key):
    return pl.pallas_call(
        value_kernel,
        out_shape=(jax.ShapeDtypeStruct((CHUNKS, CHUNK, HEAD), BF16), jax.ShapeDtypeStruct((4, HEADS, UNIT), F32)),
        in_specs=[SM, ANY, ANY],
        out_specs=(ANY, VM),
        scratch_shapes=[
            pltpu.VMEM((4, UNIT, WIDE), BF16),
            pltpu.VMEM((2 * CHUNKS, UNIT, HEAD), BF16),
            pltpu.VMEM((MAX_CHUNKS, CHUNK, ROWS), F32),
            pltpu.VMEM((MAX_CHUNKS, CHUNK, ROWS), BF16),
            pltpu.VMEM((HEAD, ROWS), BF16),
            pltpu.VMEM((ROWS, HEAD), BF16),
            pltpu.VMEM((CHUNKS, CHUNK, HEAD), F32),
            pltpu.VMEM((CHUNKS, CHUNK, HEAD), BF16),
            pltpu.VMEM((8, ROWS), F32),
            pltpu.VMEM((8, ROWS), F32),
            pltpu.SemaphoreType.DMA((4,)),
            pltpu.SemaphoreType.DMA((2 * CHUNKS,)),
            pltpu.SemaphoreType.DMA((CHUNKS,)),
        ],
        compiler_params=pltpu.CompilerParams(vmem_limit_bytes=VMEM_LIMIT),
        cost_estimate=pl.CostEstimate(flops=7_000_000_000, bytes_accessed=5_000_000, transcendentals=6_000_000),
    )(info, parts, key)


def key_kernel(info, p_ref, k_ref, v_ref, lse_ref, q0, q1, q2, q3, dk_ref, part, key, value, qn, qt, gn, lse, dq, dqs, dk, out, in_sems, key_sems, value_sems, out_sems, q_sems):
    x = info[0]
    z = info[1]
    load_key = load_units(k_ref, key, key_sems)
    load_value = load_units(v_ref, value, value_sems, pl.ds(0, HEAD))
    load_part = load_parts(p_ref, part, in_sems)
    dk[...] = jnp.zeros_like(dk)

    def minus(ch, carry):
        value[ch, :, HEAD : 2 * HEAD] = jnp.full((UNIT, HEAD), -1.0, BF16)
        return carry

    lax.fori_loop(0, 2 * CHUNKS, minus, 0)
    for copy in load_key + load_value:
        copy.wait()
    lane = lax.broadcasted_iota(jnp.int32, (UNIT, HEAD), 1)

    def put(unit):
        return pltpu.make_async_copy(out.at[unit], dk_ref.at[unit], out_sems.at[unit])

    def one_tile(t, carry):
        i = 3 - t
        unit = 8 * i + z
        lo = info[2 + i]
        hi = unit // 2
        load_part(i).wait()
        extra = part[i, :, 2 * ROWS : WIDE]
        for h in range(HEADS):
            rows = slice(h * UNIT, (h + 1) * UNIT)
            block = part[i, :, h * HEAD : (h + 1) * HEAD]
            qn[rows, :] = block
            qt[:, rows] = block.T
            gn[rows, 0:HEAD] = part[i, :, ROWS + h * HEAD : ROWS + (h + 1) * HEAD]
            gn[rows, HEAD : 2 * HEAD] = jnp.where(lane % HEADS == h, extra, jnp.zeros_like(extra))
            lse[rows, :] = jnp.broadcast_to(lse_ref[i, h : h + 1, :], (UNIT, HEAD)).T
        dq[...] = jnp.zeros_like(dq)

        def gradients(chs, mask=False):
            ss = [dot(qn[...], chunks(key, ch), NT) for ch in chs]
            dps = [dot(gn[...], chunks(value, ch), NT).astype(BF16) for ch in chs]
            if mask:
                row = lax.broadcasted_iota(jnp.int32, (ROWS, CHUNK), 0) % UNIT + (unit % 2) * UNIT
                col = lax.broadcasted_iota(jnp.int32, (ROWS, CHUNK), 1)
                ss = [jnp.where(col <= row, s, -1e30) for s in ss]
            total = None
            for ch, s, dp in zip(chs, ss, dps):
                both = jnp.concatenate([lse[...], lse[...]], axis=1)
                ds = jnp.exp2(s * (SCALE * LOG2E) - both).astype(BF16) * dp
                dk[ch] += dot(qt[...], ds)
                one = dot(ds, chunks(key, ch))
                total = one if total is None else total + one
            dq[...] += total

        gradients((hi,), True)
        pairwise(lo, hi, gradients)
        for h in range(HEADS):
            dqs[i, :, h * HEAD : (h + 1) * HEAD] = (dq[h * UNIT : (h + 1) * UNIT, :] * SCALE).astype(BF16)

        def flush(ch, carry):
            for half in range(2):
                out[2 * ch + half] = (dk[ch, :, half * UNIT : (half + 1) * UNIT] * SCALE).astype(BF16)
                put(2 * ch + half).start()
            return carry

        lax.fori_loop(4 * i, 4 * i + 4, flush, 0)
        return carry

    lax.fori_loop(0, 4, one_tile, 0)
    copies = []
    for s, ref in enumerate((q0, q1, q2, q3)):
        copies.append(pltpu.make_async_copy(dqs.at[lax.rem(x + s, 4)], ref, q_sems.at[s]))
        copies[s].start()
    for copy in copies:
        copy.wait()

    def finish(unit, carry):
        put(unit).wait()
        return carry

    lax.fori_loop(0, 2 * CHUNKS, finish, 0)


def key_grads(info, parts, key, value, lse):
    one = jax.ShapeDtypeStruct((UNIT, ROWS), BF16)
    return pl.pallas_call(
        key_kernel,
        out_shape=[one] * 4 + [jax.ShapeDtypeStruct((2 * CHUNKS, HEAD, UNIT), BF16)],
        in_specs=[SM, ANY, ANY, ANY, VM],
        out_specs=[ANY] * 5,
        scratch_shapes=[
            pltpu.VMEM((4, UNIT, WIDE), BF16),
            pltpu.VMEM((2 * CHUNKS, UNIT, HEAD), BF16),
            pltpu.VMEM((2 * CHUNKS, UNIT, 2 * HEAD), BF16),
            pltpu.VMEM((ROWS, HEAD), BF16),
            pltpu.VMEM((HEAD, ROWS), BF16),
            pltpu.VMEM((ROWS, 2 * HEAD), BF16),
            pltpu.VMEM((ROWS, HEAD), F32),
            pltpu.VMEM((ROWS, HEAD), F32),
            pltpu.VMEM((4, UNIT, ROWS), BF16),
            pltpu.VMEM((CHUNKS, HEAD, CHUNK), F32),
            pltpu.VMEM((2 * CHUNKS, HEAD, UNIT), BF16),
            pltpu.SemaphoreType.DMA((4,)),
            pltpu.SemaphoreType.DMA((2 * CHUNKS,)),
            pltpu.SemaphoreType.DMA((2 * CHUNKS,)),
            pltpu.SemaphoreType.DMA((2 * CHUNKS,)),
            pltpu.SemaphoreType.DMA((4,)),
        ],
        compiler_params=pltpu.CompilerParams(vmem_limit_bytes=VMEM_LIMIT),
        cost_estimate=pl.CostEstimate(flops=9_000_000_000, bytes_accessed=6_000_000, transcendentals=6_000_000),
    )(info, parts, key, value, lse)


def add_senders(in_ref, out_ref, transposed):
    for c in range(4):
        total = in_ref[8 * c].astype(F32)
        for t in range(1, 8):
            total = total + in_ref[8 * c + t].astype(F32)
        if transposed:
            total = total.T
        out_ref[:, c * HEAD : (c + 1) * HEAD] = total.astype(BF16)


def sum_kernel(in_ref, out_ref):
    add_senders(in_ref, out_ref, False)


def sum_senders(parts):
    return pl.pallas_call(
        sum_kernel,
        out_shape=jax.ShapeDtypeStruct((UNIT, 4 * HEAD), BF16),
        in_specs=[VM],
        out_specs=VM,
        compiler_params=pltpu.CompilerParams(vmem_limit_bytes=8 * 1024 * 1024),
        cost_estimate=pl.CostEstimate(flops=1_000_000, bytes_accessed=1_200_000, transcendentals=0),
    )(parts)


def finish_kernel(info, q0, q1, q2, q3, dk_ref, q_ref, out_ref, sems):
    copies = []
    for s, ref in enumerate((q0, q1, q2, q3)):
        base = pl.multiple_of(lax.rem(info[0] + 4 - s, 4) * ROWS, ROWS)
        copies.append(pltpu.make_async_copy(ref, q_ref.at[:, pl.ds(base, ROWS)], sems.at[s]))
        copies[s].start()
    add_senders(dk_ref, out_ref, True)
    for copy in copies:
        copy.wait()


def finish(info, dq, dk):
    return pl.pallas_call(
        finish_kernel,
        out_shape=(jax.ShapeDtypeStruct((UNIT, 4 * ROWS), BF16), jax.ShapeDtypeStruct((UNIT, 4 * HEAD), BF16)),
        in_specs=[SM] + [VM] * 5,
        out_specs=(ANY, VM),
        scratch_shapes=[pltpu.SemaphoreType.DMA((4,))],
        compiler_params=pltpu.CompilerParams(vmem_limit_bytes=8 * 1024 * 1024),
        cost_estimate=pl.CostEstimate(flops=1_000_000, bytes_accessed=3_000_000, transcendentals=0),
    )(info, *dq, dk)


def shift(array, by):
    return lax.ppermute(array, "x", [(i, (i + by) % 4) for i in range(4)])


def exchange(parts):
    return [parts[0]] + [shift(parts[s], s) for s in (1, 2, 3)]


def to_all(array):
    return lax.all_to_all(array, ("x", "z"), 0, 0, tiled=True)


def on_device(queries, keys, values, outputs, out_grad, doc_start):
    x = lax.axis_index("x")
    z = lax.axis_index("z")
    own_start = lax.dynamic_index_in_dim(doc_start, lax.axis_index("dp"), 0, keepdims=False)
    first_chunk = own_start.reshape(4, 8, UNIT)[:, :, 0] // CHUNK
    first_chunk = lax.dynamic_index_in_dim(first_chunk, z, 1, keepdims=False)
    info = jnp.concatenate([x[None].astype(jnp.int32), z[None].astype(jnp.int32), first_chunk])

    kv = lax.all_to_all(pack_keys(keys, values).astype(jnp.float16), "x", 0, 0, tiled=True)
    parts = lax.all_to_all(pack(queries, outputs, out_grad), "x", 0, 0, tiled=True)
    kv = lax.all_gather(kv, "z", axis=0)
    key, value = unpack(kv, 0), unpack(kv, 1)
    dv, lse = value_grads(info, parts, key)
    dv = to_all(dv.reshape(32, UNIT, HEAD))
    *dq, dk = key_grads(info, parts, key, value, lse)
    dk, dv = lax.optimization_barrier((dk, dv))
    dk = to_all(dk)
    dq = exchange(dq)
    value_gradient = sum_senders(dv)
    dq, value_gradient = lax.optimization_barrier((dq, value_gradient))
    q_grad, key_gradient = finish(info, dq, dk)
    return q_grad, key_gradient, value_gradient


def solution(mesh):
    split = Mesh(mesh.devices.reshape(16, 4, 8), ("dp", "x", "z"))
    rows = P(("dp", "x", "z"), None)
    return jax.shard_map(
        on_device,
        mesh=split,
        in_specs=(rows, rows, rows, rows, rows, P()),
        out_specs=(rows, rows, rows),
        check_vma=False,
    )
```
